32 devices in a mesh: dp: 4 (over z), node: 8 (over y, x, core).
Axes of the slice: x: 2, y: 2, z: 4, core: 2. Of those that a mesh axis runs over, the one named last changes fastest.
Arguments:
- vertex_embeddings: bfloat16 [4, 4096, 768], P('dp', 'node'), may hold values from -12 to 12
- incoming_adjoint: bfloat16 [4, 4096, 768], P('dp', 'node'), may hold values from -6 to 6
- asking_projector_matrix: bfloat16 [768, 768], replicated, may hold values from -0.21875 to 0.21875
- lookup_projector_matrix: bfloat16 [768, 768], replicated, may hold values from -0.21875 to 0.21875
- content_projector_matrix: bfloat16 [768, 768], replicated, may hold values from -0.21875 to 0.21875
- final_projector_matrix: bfloat16 [768, 768], replicated, may hold values from -0.21875 to 0.21875
- grouped_vertex_permutation: int32 [4, 4096], P('dp'), may hold values from 0 to 4095, as said below
- listed_tiles: int32 [4, 32, 32, 4], P('dp'), may hold values from 0 to 31, as said below
- active_tile_tally: int32 [4, 32, 32], P('dp'), may hold values from 1 to 4, as said below
Outputs:
- sublayer_yield: bfloat16 [4, 4096, 768], P('dp', 'node')
- embedding_derivative: bfloat16 [4, 4096, 768], P('dp', 'node')
- grad_query: float32 [768, 768], replicated
- grad_key: float32 [768, 768], replicated
- grad_value: float32 [768, 768], replicated
- grad_out: float32 [768, 768], replicated
The draws below stay inside these ranges and needn't reach their ends.
Inputs may be any that keep to these rules, and one draw needn't show every extreme that they name: `grouped_vertex_permutation`: each subgraph's row is a permutation of the 4096 nodes. listed_tiles[g, h, b, :] are 4 distinct key block numbers, the first of them b. `active_tile_tally`: for every subgraph and head some query block has 4.
All inputs are finite; a program needn't handle non-finite values.
Results may differ from the reference program's by a relative error of at most 0.015.
The reference program's roundings to bfloat16 on the way count: a program that leaves them out, or rounds other values in their place, can miss the bound.
Values may be sent and summed in bfloat16 or wider, within the bound.
A program may use at most 128 MiB of HBM per device.

```python
import math
import jax
import jax.numpy as jnp
from jax import lax

H = 32
HD = 24
BLOCK = 128
MAXB = 4
D = 768
G = 4
N = 4096
NB = 32


def order_table(key):
    base = jax.random.fold_in(key, 11)
    keys = jax.random.split(base, G)
    return jax.vmap(lambda one: jax.random.permutation(one, N))(keys).astype(jnp.int32)


def draw_grouped_vertex_permutation(key, part):
    return order_table(key)


def draw_vertex_embeddings(key, part):
    order = order_table(key)
    noise_key, offset_key, strength_key = jax.random.split(jax.random.fold_in(key, 23), 3)
    offsets = jax.random.randint(offset_key, (G, NB, 2), 0, BLOCK)
    lane = jnp.arange(BLOCK, dtype=jnp.int32)
    marked = jnp.any(lane[None, None, None, :] == offsets[..., None], axis=2)
    marked = marked.reshape(G, N).astype(jnp.float32)
    placed = jax.vmap(lambda where, flags: jnp.zeros((N,), jnp.float32).at[where].set(flags))(order, marked)
    base = jnp.clip(jax.random.normal(noise_key, (G, N, D), jnp.float32), -2.5, 2.5)
    strength = jnp.exp(jax.random.uniform(strength_key, (G, N), jnp.float32, math.log(1.5), math.log(3.0)))
    drawn = jnp.ones((G, N), jnp.float32)
    score_scale = drawn + placed * (strength - drawn)
    return (base * score_scale[..., None]).astype(jnp.bfloat16)


def draw_listed_tiles(key, part):
    raw = jax.random.randint(key, (G, H, NB, NB), 0, 1 << 20)
    cols = jnp.arange(NB, dtype=jnp.int32)
    score = raw * NB + cols[None, None, None, :]
    own = cols[:, None] == cols[None, :]
    score = jnp.where(own[None, None, :, :], 1 << 30, score)
    picked = lax.top_k(score, MAXB)[1]
    return picked.astype(jnp.int32)


def draw_active_tile_tally(key, part):
    first, second = jax.random.split(key)
    base = jax.random.randint(first, (G, H, NB), 1, MAXB + 1)
    where_full = jax.random.randint(second, (G, H, 1), 0, NB)
    cols = jnp.arange(NB, dtype=jnp.int32)[None, None, :]
    return jnp.where(cols == where_full, MAXB, base).astype(jnp.int32)


def levels(own_key, shape, cuts, least, high):
    loudness, own = 1.0, jax.random.fold_in(own_key, 6)
    for dim, shards_of in cuts:
        steps = jnp.exp(jax.random.uniform(jax.random.fold_in(own, dim), (shards_of,), jnp.float32, least / len(cuts), high / len(cuts)))
        loudness = loudness * jnp.repeat(steps, shape[dim] // shards_of).reshape([-1 if axis == dim else 1 for axis in range(len(shape))])
    return loudness


def noise(rng, dims, deviation, reach, pieces=(), held_as=jnp.bfloat16):
    array = deviation * jax.random.normal(rng, dims, jnp.float32)
    if pieces:
        array = array * levels(rng, dims, pieces, -0.22, 0.18)
    return jnp.clip(array, -reach, reach).astype(held_as)


def setup_inputs(seed: int = 0) -> dict:
    streams_of = jax.random.split(jax.random.key(seed), 10)
    return {
        "vertex_embeddings": draw_vertex_embeddings(jax.random.fold_in(streams_of[9], 71), 0),
        "incoming_adjoint": noise(streams_of[1], (G, N, D), 1.0, 6.0, ((0, 4), (1, 8))),
        "asking_projector_matrix": noise(streams_of[2], (D, D), D ** -0.5, 0.21875),
        "lookup_projector_matrix": noise(streams_of[3], (D, D), D ** -0.5, 0.21875),
        "content_projector_matrix": noise(streams_of[4], (D, D), D ** -0.5, 0.21875),
        "final_projector_matrix": noise(streams_of[5], (D, D), D ** -0.5, 0.21875),
        "grouped_vertex_permutation": draw_grouped_vertex_permutation(jax.random.fold_in(streams_of[9], 71), 0),
        "listed_tiles": draw_listed_tiles(jax.random.fold_in(streams_of[9], 71), 0),
        "active_tile_tally": draw_active_tile_tally(jax.random.fold_in(streams_of[9], 71), 0),
    }


def head_pass(args):
    qh, kh, vh, doh, ids, cnt = args
    block_count, neighbor_slots = ids.shape
    block_slice = qh.shape[0] // block_count
    head_width = qh.shape[1]
    score_scale = 1.0 / math.sqrt(head_width)
    query_block = qh.reshape(block_count, block_slice, head_width).astype(jnp.float32)
    key_gathered = kh.reshape(block_count, block_slice, head_width)[ids].reshape(block_count, neighbor_slots * block_slice, head_width).astype(jnp.float32)
    value_gathered = vh.reshape(block_count, block_slice, head_width)[ids].reshape(block_count, neighbor_slots * block_slice, head_width).astype(jnp.float32)
    output_gradient_block = doh.reshape(block_count, block_slice, head_width).astype(jnp.float32)
    score_block = jnp.einsum('fce,fte->fct', query_block, key_gathered) * score_scale
    live = (jnp.arange(neighbor_slots * block_slice) // block_slice)[None, None, :] < cnt[:, None, None]
    score_block = jnp.where(live, score_block, -1e+30)
    top = lax.optimization_barrier(jnp.max(score_block, axis=-1, keepdims=True))
    expo = jnp.exp(score_block - top)
    prob = expo / lax.optimization_barrier(jnp.sum(expo, axis=-1, keepdims=True))
    probability_block = prob.astype(jnp.bfloat16).astype(jnp.float32)
    output_rows = jnp.einsum('xow,xwv->xov', probability_block, value_gathered).astype(jnp.bfloat16)
    probability_gradient = jnp.einsum('fce,fte->fct', output_gradient_block, value_gathered)
    delta = lax.optimization_barrier(jnp.sum(prob * probability_gradient, axis=-1, keepdims=True))
    score_gradient = (prob * (probability_gradient - delta) * score_scale).astype(jnp.bfloat16).astype(jnp.float32)
    query_gradient = jnp.einsum('xow,xwv->xov', score_gradient, key_gathered)
    key_gradient_gathered = jnp.einsum('wjh,wjs->whs', score_gradient, query_block).reshape(block_count, neighbor_slots, block_slice, head_width)
    value_gradient_gathered = jnp.einsum('wjh,wjs->whs', probability_block, output_gradient_block).reshape(block_count, neighbor_slots, block_slice, head_width)
    dk = jnp.zeros((block_count, block_slice, head_width), jnp.float32).at[ids].add(key_gradient_gathered)
    dv = jnp.zeros((block_count, block_slice, head_width), jnp.float32).at[ids].add(value_gradient_gathered)
    total = block_count * block_slice
    return (output_rows.reshape(total, head_width), query_gradient.reshape(total, head_width), dk.reshape(total, head_width), dv.reshape(total, head_width))

def partition_tiles(asking_projector_matrix, lookup_projector_matrix, content_projector_matrix, final_projector_matrix):

    def run(args):
        xg, dyg, order, ids, cnt = args
        q = jnp.dot(xg, asking_projector_matrix, preferred_element_type=jnp.float32).astype(jnp.bfloat16)
        k = jnp.dot(xg, lookup_projector_matrix, preferred_element_type=jnp.float32).astype(jnp.bfloat16)
        v = jnp.dot(xg, content_projector_matrix, preferred_element_type=jnp.float32).astype(jnp.bfloat16)
        upstream = jnp.dot(dyg, final_projector_matrix.T, preferred_element_type=jnp.float32).astype(jnp.bfloat16)

        def heads_of(a):
            return a[order].reshape(N, H, HD).transpose(1, 0, 2)
        res = lax.map(head_pass, (heads_of(q), heads_of(k), heads_of(v), heads_of(upstream), ids, cnt))

        def restore(a, dtype):
            flat = a.transpose(1, 0, 2).reshape(N, H * HD).astype(dtype)
            return jnp.zeros((N, H * HD), dtype).at[order].set(flat)
        output_rows = restore(res[0], jnp.bfloat16)
        query_gradient = restore(res[1], jnp.bfloat16)
        dk = restore(res[2], jnp.bfloat16)
        dv = restore(res[3], jnp.bfloat16)
        result = jnp.dot(output_rows, final_projector_matrix, preferred_element_type=jnp.float32).astype(jnp.bfloat16)
        back = (jnp.dot(query_gradient, asking_projector_matrix.T, preferred_element_type=jnp.float32) + jnp.dot(dk, lookup_projector_matrix.T, preferred_element_type=jnp.float32) + jnp.dot(dv, content_projector_matrix.T, preferred_element_type=jnp.float32)).astype(jnp.bfloat16)
        derivative_bundle = jnp.stack([jnp.dot(xg.T, query_gradient, preferred_element_type=jnp.float32), jnp.dot(xg.T, dk, preferred_element_type=jnp.float32), jnp.dot(xg.T, dv, preferred_element_type=jnp.float32), jnp.dot(output_rows.T, dyg, preferred_element_type=jnp.float32)])
        return (result, back, derivative_bundle)
    return run

def reference(vertex_embeddings, incoming_adjoint, asking_projector_matrix, lookup_projector_matrix, content_projector_matrix, final_projector_matrix, grouped_vertex_permutation, listed_tiles, active_tile_tally):
    sublayer_yield, embedding_derivative, derivative_bundle = lax.map(partition_tiles(asking_projector_matrix, lookup_projector_matrix, content_projector_matrix, final_projector_matrix), (vertex_embeddings, incoming_adjoint, grouped_vertex_permutation, listed_tiles, active_tile_tally))
    factor = 1.0 / math.sqrt(G * N)
    summed = lax.optimization_barrier(jnp.sum(derivative_bundle, axis=0)) * factor
    return (sublayer_yield, embedding_derivative, summed[0], summed[1], summed[2], summed[3])
```

```python
import functools
import math

import jax
import jax.numpy as jnp
from jax import lax
from jax.experimental import pallas as pl
from jax.experimental.pallas import tpu as pltpu
from jax.sharding import PartitionSpec as P

H = 32
HD = 24
BLOCK = 128
WIDE = 2 * BLOCK
F32 = jnp.float32
BF16 = jnp.bfloat16


def attention_kernel(
    heads, slots, ids_ref, cnt_ref, row_ref, col_ref, a_ref, out_ref, vkt, vkn, rhs, acc, odq, packed
):
    sources, _, chunk = a_ref.shape
    nblocks = vkt.shape[1]
    per_chunk = chunk // BLOCK
    scale = 1.0 / math.sqrt(HD)
    to_exp2 = scale * math.log2(math.e)
    zero = jnp.zeros((HD, BLOCK), F32)

    def reorder(turn, carry):
        row = row_ref[turn]
        place = lax.broadcasted_iota(jnp.int32, (chunk, WIDE), 0)
        total = None
        for s in range(sources):
            onehot = jnp.where(place == row - s * chunk, 1.0, 0.0).astype(BF16)
            part = jnp.dot(a_ref[s], onehot, preferred_element_type=F32)
            total = part if total is None else total + part
        for h in range(heads):
            for half in range(2):
                b = turn * 2 + half
                base = h * 4 * HD
                lanes = slice(half * BLOCK, (half + 1) * BLOCK)
                vk = total[base : base + 2 * HD, lanes]
                up = total[base + 2 * HD : base + 3 * HD, lanes]
                q = total[base + 3 * HD : base + 4 * HD, lanes]
                vkt[h, b] = vk.astype(BF16)
                vkn[h, b] = vk.T.astype(BF16)
                rhs[h, b] = jnp.concatenate(
                    [
                        jnp.concatenate([up, zero], axis=1),
                        jnp.concatenate([zero, q], axis=1),
                    ],
                    axis=0,
                ).astype(BF16)
                acc[h, b] = jnp.zeros((2 * HD, BLOCK), F32)
        return carry

    lax.fori_loop(0, nblocks // 2, reorder, 0)

    def attend(b, carry):
        for h in range(heads):
            first = (h * nblocks + b) * slots
            ids = [ids_ref[first + m] for m in range(slots)]
            count = cnt_ref[h * nblocks + b]
            right = rhs[h, b]
            both = []
            for m in range(slots):
                both.append(jnp.dot(vkn[h, ids[m]], right, preferred_element_type=F32))
            score = [
                jnp.where(m < count, both[m][:, BLOCK:], -1e30) for m in range(slots)
            ]
            top = functools.reduce(
                jnp.maximum, [jnp.max(s, axis=0, keepdims=True) for s in score]
            )
            expo = [jnp.exp2((s - top) * to_exp2) for s in score]
            norm = sum(jnp.sum(e, axis=0, keepdims=True) for e in expo)
            inv = 1.0 / norm
            prob = [e * inv for e in expo]
            grad = [both[m][:, :BLOCK] for m in range(slots)]
            delta = sum(
                jnp.sum(prob[m] * grad[m], axis=0, keepdims=True) for m in range(slots)
            )
            pd = jnp.concatenate(
                [
                    jnp.concatenate(
                        [
                            prob[m].astype(BF16),
                            (prob[m] * (grad[m] - delta) * scale).astype(BF16),
                        ],
                        axis=1,
                    )
                    for m in range(slots)
                ],
                axis=0,
            )
            left = jnp.concatenate([vkt[h, ids[m]] for m in range(slots)], axis=1)
            forward = jnp.dot(left, pd, preferred_element_type=F32)
            odq[h, b] = jnp.concatenate([forward[:HD, :BLOCK], forward[HD:, BLOCK:]], axis=0)
            back = lax.dot_general(
                right, pd, (((1,), (1,)), ((), ())), preferred_element_type=F32
            )
            for m in range(slots):
                acc[h, ids[m]] += back[:, m * BLOCK : (m + 1) * BLOCK]
        return carry

    lax.fori_loop(0, nblocks, attend, 0)

    def pack(g, carry):
        for j in range(per_chunk):
            b = g * per_chunk + j
            pieces = [odq[h, b, :HD] for h in range(heads)]
            pieces += [odq[h, b, HD:] for h in range(heads)]
            pieces += [acc[h, b, :HD] for h in range(heads)]
            pieces += [acc[h, b, HD:] for h in range(heads)]
            packed[g, :, j * BLOCK : (j + 1) * BLOCK] = jnp.concatenate(pieces, axis=0).astype(BF16)
        return carry

    lax.fori_loop(0, sources, pack, 0)

    def restore(s, carry):
        lane = lax.broadcasted_iota(jnp.int32, (chunk, BLOCK), 1)
        for part in range(chunk // WIDE):
            low = lane + (s * chunk + part * WIDE)
            high = low + BLOCK
            total = None
            for g in range(sources):
                col = col_ref[g * chunk : (g + 1) * chunk]
                onehot = jnp.concatenate(
                    [
                        jnp.where(col == low, 1.0, 0.0).astype(BF16),
                        jnp.where(col == high, 1.0, 0.0).astype(BF16),
                    ],
                    axis=1,
                )
                got = jnp.dot(packed[g], onehot, preferred_element_type=F32)
                total = got if total is None else total + got
            out_ref[s, :, part * WIDE : (part + 1) * WIDE] = total.astype(BF16)
        return carry

    lax.fori_loop(0, sources, restore, 0)


def attention(ids, counts, order, arrived, heads):
    sources, rows, chunk = arrived.shape
    total = order.shape[0]
    nblocks = total // BLOCK
    slots = ids.shape[-1]
    vmem = pl.BlockSpec(memory_space=pltpu.VMEM)
    smem = pl.BlockSpec(memory_space=pltpu.SMEM)
    return pl.pallas_call(
        functools.partial(attention_kernel, heads, slots),
        out_shape=jax.ShapeDtypeStruct((sources, rows, chunk), BF16),
        in_specs=[smem, smem, vmem, vmem, vmem],
        out_specs=vmem,
        scratch_shapes=[
            pltpu.VMEM((heads, nblocks, 2 * HD, BLOCK), BF16),
            pltpu.VMEM((heads, nblocks, BLOCK, 2 * HD), BF16),
            pltpu.VMEM((heads, nblocks, 2 * HD, WIDE), BF16),
            pltpu.VMEM((heads, nblocks, 2 * HD, BLOCK), F32),
            pltpu.VMEM((heads, nblocks, 2 * HD, BLOCK), F32),
            pltpu.VMEM((sources, rows, chunk), BF16),
        ],
        compiler_params=pltpu.CompilerParams(vmem_limit_bytes=52 * 1024 * 1024),
        cost_estimate=pl.CostEstimate(
            flops=60_000_000_000, bytes_accessed=100_000_000, transcendentals=0
        ),
        name="attention",
    )(
        ids.reshape(-1),
        counts.reshape(-1),
        order.reshape(total // WIDE, 1, WIDE),
        jnp.broadcast_to(order[:, None], (total, BLOCK)),
        arrived,
    )


def project(weight, rows):
    return lax.dot_general(
        weight, rows, (((0,), (1,)), ((), ())), preferred_element_type=F32
    ).astype(BF16)


def local(
    vertex_embeddings,
    incoming_adjoint,
    asking_projector_matrix,
    lookup_projector_matrix,
    content_projector_matrix,
    final_projector_matrix,
    grouped_vertex_permutation,
    listed_tiles,
    active_tile_tally,
):
    rows = vertex_embeddings[0]
    cotan = incoming_adjoint[0]
    parts = lax.axis_size("node")
    groups = lax.axis_size("dp")
    heads = H // parts
    feats = heads * HD
    chunk, width = rows.shape
    order = grouped_vertex_permutation[0]
    total = order.shape[0]

    pq = project(asking_projector_matrix, rows)
    pk = project(lookup_projector_matrix, rows)
    pv = project(content_projector_matrix, rows)
    up = lax.dot_general(
        final_projector_matrix, cotan, (((1,), (1,)), ((), ())), preferred_element_type=F32
    ).astype(BF16)
    outgoing = jnp.stack(
        [x.reshape(parts, heads, HD, chunk) for x in (pv, pk, up, pq)], axis=2
    ).reshape(parts, 4 * feats, chunk)
    arrived = lax.all_to_all(outgoing, "node", split_axis=0, concat_axis=0, tiled=True)
    all_rows = lax.all_gather(rows, "node", axis=0, tiled=True)
    all_cotan = lax.all_gather(cotan, "node", axis=0, tiled=True)

    first = lax.axis_index("node") * heads
    lists = lax.dynamic_slice_in_dim(listed_tiles[0], first, heads, 0)
    counts = lax.dynamic_slice_in_dim(active_tile_tally[0], first, heads, 0)
    mine = attention(lists, counts, order, arrived, heads)

    got = lax.all_to_all(mine, "node", split_axis=0, concat_axis=0, tiled=True)
    got = got.reshape(parts, 4, feats, chunk)

    by_type = mine.reshape(parts, 4, feats, chunk)
    grads = by_type[:, 1:].transpose(1, 2, 0, 3).reshape(3 * feats, total)
    outs = by_type[:, 0].transpose(1, 0, 2).reshape(feats, total)
    partial = jnp.concatenate(
        [
            jnp.dot(outs, all_cotan, preferred_element_type=F32).astype(BF16),
            jnp.dot(grads, all_rows, preferred_element_type=F32).astype(BF16),
        ],
        axis=0,
    ).reshape(groups, 4 * feats // groups, width)
    shares = lax.all_to_all(partial, "dp", split_axis=0, concat_axis=0, tiled=True)
    share = jnp.sum(shares.astype(F32), axis=0).astype(BF16)
    summed = lax.all_gather(share, ("node", "dp"), axis=0, tiled=True)
    summed = summed.reshape(parts, 4, feats, width)
    factor = 1.0 / math.sqrt(groups * total)

    def whole(which):
        return summed[:, which].reshape(parts * feats, width)

    grad_out = whole(0).astype(F32) * factor
    grad_query = whole(1).T.astype(F32) * factor
    grad_value = whole(2).T.astype(F32) * factor
    grad_key = whole(3).T.astype(F32) * factor

    def nodes(which):
        return got[:, which].reshape(parts * feats, chunk)

    dims_first = (((0,), (0,)), ((), ()))
    dims_back = (((0,), (1,)), ((), ()))
    result = lax.dot_general(
        nodes(0), final_projector_matrix, dims_first, preferred_element_type=F32
    ).astype(BF16)
    backward = (
        lax.dot_general(nodes(1), asking_projector_matrix, dims_back, preferred_element_type=F32)
        + lax.dot_general(nodes(3), lookup_projector_matrix, dims_back, preferred_element_type=F32)
        + lax.dot_general(nodes(2), content_projector_matrix, dims_back, preferred_element_type=F32)
    ).astype(BF16)
    return (result[None], backward[None], grad_query, grad_key, grad_value, grad_out)


def solution(mesh):
    placed = (
        P("dp", "node", None),
        P("dp", "node", None),
        P(),
        P(),
        P(),
        P(),
        P("dp", None),
        P("dp", None, None, None),
        P("dp", None, None),
    )
    return jax.shard_map(
        local,
        mesh=mesh,
        in_specs=placed,
        out_specs=(P("dp", "node", None), P("dp", "node", None), P(), P(), P(), P()),
        check_vma=False,
    )
```

```python
import functools
import math

import jax
import jax.numpy as jnp
from jax import lax
from jax.experimental import pallas as pl
from jax.experimental.pallas import tpu as pltpu
from jax.sharding import PartitionSpec as P

H = 32
HD = 24
BLOCK = 128
WIDE = 2 * BLOCK
F32 = jnp.float32
BF16 = jnp.bfloat16


def attention_kernel(
    heads, slots, ids_ref, cnt_ref, row_ref, col_ref, a_ref, out_ref, vkt, vkn, rhs, acc, odq, packed
):
    sources, _, chunk = a_ref.shape
    nblocks = vkt.shape[1]
    per_chunk = chunk // BLOCK
    scale = 1.0 / math.sqrt(HD)
    to_exp2 = scale * math.log2(math.e)
    zero = jnp.zeros((HD, BLOCK), F32)

    def reorder(turn, carry):
        row = row_ref[turn]
        place = lax.broadcasted_iota(jnp.int32, (chunk, WIDE), 0)
        total = None
        for s in range(sources):
            onehot = jnp.where(place == row - s * chunk, 1.0, 0.0).astype(BF16)
            part = jnp.dot(a_ref[s], onehot, preferred_element_type=F32)
            total = part if total is None else total + part
        for h in range(heads):
            for half in range(2):
                b = turn * 2 + half
                base = h * 4 * HD
                lanes = slice(half * BLOCK, (half + 1) * BLOCK)
                vk = total[base : base + 2 * HD, lanes]
                up = total[base + 2 * HD : base + 3 * HD, lanes]
                q = total[base + 3 * HD : base + 4 * HD, lanes]
                vkt[h, b] = vk.astype(BF16)
                vkn[h, b] = vk.T.astype(BF16)
                rhs[h, b] = jnp.concatenate(
                    [
                        jnp.concatenate([up, zero], axis=1),
                        jnp.concatenate([zero, q], axis=1),
                    ],
                    axis=0,
                ).astype(BF16)
                acc[h, b] = jnp.zeros((2 * HD, BLOCK), F32)
        return carry

    lax.fori_loop(0, nblocks // 2, reorder, 0)

    def attend(b, carry):
        for h in range(heads):
            first = (h * nblocks + b) * slots
            ids = [ids_ref[first + m] for m in range(slots)]
            count = cnt_ref[h * nblocks + b]
            right = rhs[h, b]
            both = []
            for m in range(slots):
                both.append(jnp.dot(vkn[h, ids[m]], right, preferred_element_type=F32))
            score = [
                jnp.where(m < count, both[m][:, BLOCK:], -1e30) for m in range(slots)
            ]
            top = functools.reduce(
                jnp.maximum, [jnp.max(s, axis=0, keepdims=True) for s in score]
            )
            expo = [jnp.exp2((s - top) * to_exp2) for s in score]
            norm = sum(jnp.sum(e, axis=0, keepdims=True) for e in expo)
            inv = 1.0 / norm
            prob = [e * inv for e in expo]
            grad = [both[m][:, :BLOCK] for m in range(slots)]
            delta = sum(
                jnp.sum(prob[m] * grad[m], axis=0, keepdims=True) for m in range(slots)
            )
            pd = jnp.concatenate(
                [
                    jnp.concatenate(
                        [
                            prob[m].astype(BF16),
                            (prob[m] * (grad[m] - delta) * scale).astype(BF16),
                        ],
                        axis=1,
                    )
                    for m in range(slots)
                ],
                axis=0,
            )
            left = jnp.concatenate([vkt[h, ids[m]] for m in range(slots)], axis=1)
            forward = jnp.dot(left, pd, preferred_element_type=F32)
            odq[h, b] = jnp.concatenate([forward[:HD, :BLOCK], forward[HD:, BLOCK:]], axis=0)
            back = lax.dot_general(
                right, pd, (((1,), (1,)), ((), ())), preferred_element_type=F32
            )
            for m in range(slots):
                acc[h, ids[m]] += back[:, m * BLOCK : (m + 1) * BLOCK]
        return carry

    lax.fori_loop(0, nblocks, attend, 0)

    def pack(g, carry):
        for j in range(per_chunk):
            b = g * per_chunk + j
            pieces = [odq[h, b, :HD] for h in range(heads)]
            pieces += [odq[h, b, HD:] for h in range(heads)]
            pieces += [acc[h, b, :HD] for h in range(heads)]
            pieces += [acc[h, b, HD:] for h in range(heads)]
            packed[g, :, j * BLOCK : (j + 1) * BLOCK] = jnp.concatenate(pieces, axis=0).astype(BF16)
        return carry

    lax.fori_loop(0, sources, pack, 0)

    def restore(s, carry):
        lane = lax.broadcasted_iota(jnp.int32, (chunk, BLOCK), 1)
        for part in range(chunk // WIDE):
            low = lane + (s * chunk + part * WIDE)
            high = low + BLOCK
            total = None
            for g in range(sources):
                col = col_ref[g * chunk : (g + 1) * chunk]
                onehot = jnp.concatenate(
                    [
                        jnp.where(col == low, 1.0, 0.0).astype(BF16),
                        jnp.where(col == high, 1.0, 0.0).astype(BF16),
                    ],
                    axis=1,
                )
                got = jnp.dot(packed[g], onehot, preferred_element_type=F32)
                total = got if total is None else total + got
            out_ref[s, :, part * WIDE : (part + 1) * WIDE] = total.astype(BF16)
        return carry

    lax.fori_loop(0, sources, restore, 0)


def attention(ids, counts, order, arrived, heads):
    sources, rows, chunk = arrived.shape
    total = order.shape[0]
    nblocks = total // BLOCK
    slots = ids.shape[-1]
    vmem = pl.BlockSpec(memory_space=pltpu.VMEM)
    smem = pl.BlockSpec(memory_space=pltpu.SMEM)
    return pl.pallas_call(
        functools.partial(attention_kernel, heads, slots),
        out_shape=jax.ShapeDtypeStruct((sources, rows, chunk), BF16),
        in_specs=[smem, smem, vmem, vmem, vmem],
        out_specs=vmem,
        scratch_shapes=[
            pltpu.VMEM((heads, nblocks, 2 * HD, BLOCK), BF16),
            pltpu.VMEM((heads, nblocks, BLOCK, 2 * HD), BF16),
            pltpu.VMEM((heads, nblocks, 2 * HD, WIDE), BF16),
            pltpu.VMEM((heads, nblocks, 2 * HD, BLOCK), F32),
            pltpu.VMEM((heads, nblocks, 2 * HD, BLOCK), F32),
            pltpu.VMEM((sources, rows, chunk), BF16),
        ],
        compiler_params=pltpu.CompilerParams(vmem_limit_bytes=52 * 1024 * 1024),
        cost_estimate=pl.CostEstimate(
            flops=60_000_000_000, bytes_accessed=100_000_000, transcendentals=0
        ),
        name="attention",
    )(
        ids.reshape(-1),
        counts.reshape(-1),
        order.reshape(total // WIDE, 1, WIDE),
        jnp.broadcast_to(order[:, None], (total, BLOCK)),
        arrived,
    )


def project(weight, rows):
    return lax.dot_general(
        weight, rows, (((0,), (1,)), ((), ())), preferred_element_type=F32
    ).astype(BF16)


def local(
    vertex_embeddings,
    incoming_adjoint,
    asking_projector_matrix,
    lookup_projector_matrix,
    content_projector_matrix,
    final_projector_matrix,
    grouped_vertex_permutation,
    listed_tiles,
    active_tile_tally,
):
    rows = vertex_embeddings[0]
    cotan = incoming_adjoint[0]
    parts = lax.axis_size("node")
    groups = lax.axis_size("dp")
    heads = H // parts
    feats = heads * HD
    chunk, width = rows.shape
    order = grouped_vertex_permutation[0]
    total = order.shape[0]

    pq = project(asking_projector_matrix, rows)
    pk = project(lookup_projector_matrix, rows)
    pv = project(content_projector_matrix, rows)
    up = lax.dot_general(
        final_projector_matrix, cotan, (((1,), (1,)), ((), ())), preferred_element_type=F32
    ).astype(BF16)
    outgoing = jnp.stack(
        [x.reshape(parts, heads, HD, chunk) for x in (pv, pk, up, pq)], axis=2
    ).reshape(parts, 4 * feats, chunk)
    arrived = lax.all_to_all(outgoing, "node", split_axis=0, concat_axis=0, tiled=True)
    arrived, late_rows, late_cotan = lax.optimization_barrier((arrived, rows, cotan))
    all_rows = lax.all_gather(late_rows, "node", axis=0, tiled=True)
    all_cotan = lax.all_gather(late_cotan, "node", axis=0, tiled=True)

    first = lax.axis_index("node") * heads
    lists = lax.dynamic_slice_in_dim(listed_tiles[0], first, heads, 0)
    counts = lax.dynamic_slice_in_dim(active_tile_tally[0], first, heads, 0)
    mine = attention(lists, counts, order, arrived, heads)

    got = lax.all_to_all(mine, "node", split_axis=0, concat_axis=0, tiled=True)
    got = got.reshape(parts, 4, feats, chunk)

    by_type = mine.reshape(parts, 4, feats, chunk)
    grads = by_type[:, 1:].transpose(1, 2, 0, 3).reshape(3 * feats, total)
    outs = by_type[:, 0].transpose(1, 0, 2).reshape(feats, total)
    partial = jnp.concatenate(
        [
            jnp.dot(outs, all_cotan, preferred_element_type=F32).astype(BF16),
            jnp.dot(grads, all_rows, preferred_element_type=F32).astype(BF16),
        ],
        axis=0,
    ).reshape(groups, 4 * feats // groups, width)
    shares = lax.all_to_all(partial, "dp", split_axis=0, concat_axis=0, tiled=True)
    share = jnp.sum(shares.astype(F32), axis=0).astype(BF16)
    summed = lax.all_gather(share, ("node", "dp"), axis=0, tiled=True)
    summed = summed.reshape(parts, 4, feats, width)
    factor = 1.0 / math.sqrt(groups * total)

    def whole(which):
        return summed[:, which].reshape(parts * feats, width)

    grad_out = whole(0).astype(F32) * factor
    grad_query = whole(1).T.astype(F32) * factor
    grad_value = whole(2).T.astype(F32) * factor
    grad_key = whole(3).T.astype(F32) * factor

    def nodes(which):
        return got[:, which].reshape(parts * feats, chunk)

    dims_first = (((0,), (0,)), ((), ()))
    dims_back = (((0,), (1,)), ((), ()))
    result = lax.dot_general(
        nodes(0), final_projector_matrix, dims_first, preferred_element_type=F32
    ).astype(BF16)
    backward = (
        lax.dot_general(nodes(1), asking_projector_matrix, dims_back, preferred_element_type=F32)
        + lax.dot_general(nodes(3), lookup_projector_matrix, dims_back, preferred_element_type=F32)
        + lax.dot_general(nodes(2), content_projector_matrix, dims_back, preferred_element_type=F32)
    ).astype(BF16)
    return (result[None], backward[None], grad_query, grad_key, grad_value, grad_out)


def solution(mesh):
    placed = (
        P("dp", "node", None),
        P("dp", "node", None),
        P(),
        P(),
        P(),
        P(),
        P("dp", None),
        P("dp", None, None, None),
        P("dp", None, None),
    )
    return jax.shard_map(
        local,
        mesh=mesh,
        in_specs=placed,
        out_specs=(P("dp", "node", None), P("dp", "node", None), P(), P(), P(), P()),
        check_vma=False,
    )
```
